32 devices in a mesh: dp: 4 (over y, core), expert: 2 (over x), seq: 4 (over z).
Axes of the slice: x: 2, y: 2, z: 4, core: 2. Of those that a mesh axis runs over, the one named last changes fastest.
Arguments:
- tokens: bfloat16 [16, 1024, 768], P(('dp', 'expert'), 'seq'), may hold values from -6 to 6
- attn_gain: float32 [768], replicated, may hold values from 0.5 to 1.5
- w_query: bfloat16 [768, 768], P(('dp', 'expert')), may hold values from -0.21875 to 0.21875
- w_key: bfloat16 [768, 768], P(('dp', 'expert')), may hold values from -0.21875 to 0.21875
- w_value: bfloat16 [768, 768], P(('dp', 'expert')), may hold values from -0.21875 to 0.21875
- output_projection_weight: bfloat16 [768, 768], P(('dp', 'expert')), may hold values from -3.5 to 3.5
- bias_table: float32 [32, 12], replicated, may hold values from -5 to 5
- rel_buckets: int32 [2047], replicated, may hold values from 0 to 31
- ffn_gain: float32 [768], replicated, may hold values from 0.5 to 1.5
- router: bfloat16 [768, 2], replicated, may hold values from -0.15625 to 0.15625
- expert_in: bfloat16 [2, 768, 3072], P('expert', 'dp'), may hold values from -0.21875 to 0.21875
- expert_out: bfloat16 [2, 3072, 768], P('expert', 'dp'), may hold values from -0.375 to 0.375
- expert_ids: int32 [16, 1024], P(('dp', 'expert'), 'seq'), may hold values from 0 to 1
- cotangent: bfloat16 [16, 1024, 768], P(('dp', 'expert'), 'seq'), may hold values from -6 to 6
Outputs:
- layer_out: bfloat16 [16, 1024, 768], P(('dp', 'expert'), 'seq')
- input_grad: float32 [16, 1024, 768], P(('dp', 'expert'), 'seq')
- attn_gain_grad: float32 [768], replicated
- query_grad: float32 [768, 768], P(('dp', 'expert'))
- key_grad: float32 [768, 768], P(('dp', 'expert'))
- value_grad: float32 [768, 768], P(('dp', 'expert'))
- output_grad: float32 [768, 768], P(('dp', 'expert'))
- table_grad: float32 [32, 12], replicated
- ffn_gain_grad: float32 [768], replicated
- router_grad: float32 [768, 2], replicated
- expert_in_grad: float32 [2, 768, 3072], P('expert', 'dp')
- expert_out_grad: float32 [2, 3072, 768], P('expert', 'dp')
The draws below stay inside these ranges and needn't reach their ends.
All inputs are finite; a program needn't handle non-finite values.
Results may differ from the reference program's by a relative error of at most 0.018.
Values may be sent and summed in bfloat16 or wider, within the bound.
A program may use at most 192 MiB of HBM per device.

```python
import math
import jax
import jax.numpy as jnp
import numpy as np
from jax import lax

D = 768
HEADS = 12
HEAD_DIM = 64
FF = 3072
BUCKETS = 32
LEN = 1024
SEQ_GRP = 2
EXPERTS = 2
SEQS = 16
TOK_DEV = 512
CAP = 320
N_DP = 4
N_EXPERT = 2
N_SEQ = 4


def set_ends(entries, own_key, smallest, top_value):
    spot = [jax.random.randint(jax.random.fold_in(own_key, axis), (), 0, length) for axis, length in enumerate(entries.shape)]
    main_axis = entries.shape.index(max(entries.shape))
    next_to = spot[:main_axis] + [(spot[main_axis] + 1) % entries.shape[main_axis]] + spot[main_axis + 1:]
    return entries.at[tuple(spot)].set(smallest).at[tuple(next_to)].set(top_value)


def steps_of(stream_key, dims, pieces, low, top_value):
    level = 1.0
    for axis_at, shards_of in pieces:
        heights = jax.random.uniform(jax.random.fold_in(jax.random.fold_in(stream_key, 6), axis_at), (shards_of,), jnp.float32, low / len(pieces), top_value / len(pieces))
        level = level * jnp.repeat(jnp.exp(heights), dims[axis_at] // shards_of).reshape((-1,) + (1,) * (len(dims) - 1 - axis_at))
    return level


def rank_table(number_of, skew):
    portions = [(1 << 20) // math.isqrt(standing ** skew) + 1 for standing in range(1, number_of + 1)]
    spread = 1 + sum(portions) // (1 << 30)
    return np.cumsum(np.array([max(1, weight // spread) for weight in portions]))


def skewed_ids(own_key, dims, count, slope):
    listing = rank_table(count, slope)
    ticket = jax.random.randint(jax.random.fold_in(own_key, 1), dims, 0, int(listing[count - 1]))
    rank = jnp.searchsorted(jnp.asarray(listing, jnp.int32), ticket, side="right")
    return jax.random.permutation(jax.random.fold_in(own_key, 2), count)[rank].astype(jnp.int32)


def gaussian(stream_key, extent, spread, bound, shards=(), dtype=jnp.bfloat16):
    values = spread * jax.random.normal(stream_key, extent, jnp.float32)
    if shards:
        values = values * steps_of(stream_key, extent, shards, -0.22, 0.18)
    return jnp.clip(values, -bound, bound).astype(dtype)


def setup_inputs(seed: int = 0) -> dict:
    key_list = jax.random.split(jax.random.key(seed), 15)
    return {
        "tokens": gaussian(key_list[0], (SEQS, LEN, D), 1.0, 6.0, ((0, 8), (1, 4))),
        "attn_gain": jnp.clip(1.0 + 0.1 * jax.random.normal(key_list[1], (D,), jnp.float32), 0.5, 1.5),
        "w_query": gaussian(key_list[2], (D, D), D ** -0.5, 0.21875, ((0, 8),)),
        "w_key": gaussian(key_list[3], (D, D), D ** -0.5, 0.21875, ((0, 8),)),
        "w_value": gaussian(key_list[4], (D, D), D ** -0.5, 0.21875, ((0, 8),)),
        "output_projection_weight": gaussian(key_list[5], (D, D), (max(D // 256, 1)) ** -0.5, 3.5, ((0, 8),)),
        "bias_table": gaussian(key_list[6], (BUCKETS, HEADS), 1.0, 5.0, (), jnp.float32),
        "rel_buckets": set_ends(jax.random.randint(key_list[7], (2 * LEN - 1,), 0, BUCKETS), jax.random.fold_in(key_list[7], 1), 0, BUCKETS - 1).astype(jnp.int32),
        "ffn_gain": jnp.clip(1.0 + 0.1 * jax.random.normal(key_list[8], (D,), jnp.float32), 0.5, 1.5),
        "router": gaussian(key_list[9], (D, EXPERTS), (2 * D) ** -0.5, 0.15625),
        "expert_in": gaussian(key_list[10], (EXPERTS, D, FF), D ** -0.5, 0.21875, ((0, 2), (1, 4))),
        "expert_out": gaussian(key_list[11], (EXPERTS, FF, D), (max(FF // (3 * EXPERTS * EXPERTS), 1)) ** -0.5, 0.375, ((0, 2), (1, 4))),
        "expert_ids": set_ends(skewed_ids(key_list[12], (SEQS, LEN), EXPERTS, 1), jax.random.fold_in(key_list[12], 3), 0, EXPERTS - 1).astype(jnp.int32),
        "cotangent": gaussian(key_list[13], (SEQS, LEN, D), 1.0, 6.0, ((0, 8), (1, 4))),
    }


eps = 1e-06
highest_precision = lax.Precision.HIGHEST

@jax.custom_vjp
def lower_precision(v):
    return lax.optimization_barrier(v.astype(jnp.bfloat16)).astype(jnp.float32)

@jax.custom_vjp
def lower_precision_backward(v):
    return v

def low_keep(v):
    return (lower_precision(v), None)

def low_pass(kept, grad):
    return (grad,)

def back_keep(v):
    return (v, None)

def back_low(kept, grad):
    return (lower_precision(grad),)
lower_precision.defvjp(low_keep, low_pass)
lower_precision_backward.defvjp(back_keep, back_low)

def normalize(residual_stream, gain):
    return residual_stream * lax.rsqrt(lax.optimization_barrier(jnp.mean(residual_stream * residual_stream, axis=-1, keepdims=True)) + eps) * gain

def device_rows(values):
    groups = N_DP * N_EXPERT
    tail = values.shape[2:]
    shaped = values.reshape((groups, SEQ_GRP, N_SEQ, LEN // N_SEQ) + tail)
    shaped = jnp.moveaxis(shaped, 2, 1)
    return shaped.reshape((groups * N_SEQ, TOK_DEV) + tail)

def from_device_rows(values):
    groups = N_DP * N_EXPERT
    tail = values.shape[2:]
    shaped = values.reshape((groups, N_SEQ, SEQ_GRP, LEN // N_SEQ) + tail)
    shaped = jnp.moveaxis(shaped, 1, 2)
    return shaped.reshape((SEQS, LEN) + tail)

def forward(residual_stream, attn_gain, w_query, w_key, w_value, output_projection_weight, bias_table, ffn_gain, router, expert_in, expert_out, rel_buckets, expert_ids):
    first_layer_norm = lower_precision(normalize(residual_stream, attn_gain))

    def project(weight_matrix):
        return lower_precision_backward(lower_precision(jnp.einsum('qxm,my->qxy', first_layer_norm, weight_matrix, precision=highest_precision)))
    query_rows, key_rows, value_rows = (project(w_query), project(w_key), project(w_value))
    rel_values = bias_table[rel_buckets]
    positions = jnp.arange(LEN)[None, :] - jnp.arange(LEN)[:, None] + LEN - 1
    bias = jnp.transpose(rel_values[positions], (2, 0, 1))
    factor = 1.0 / jnp.sqrt(jnp.float32(HEAD_DIM))

    def attend(inputs):
        query_seq, key_seq, value_seq = inputs
        query_seq = query_seq.reshape(LEN, HEADS, HEAD_DIM)
        key_seq = key_seq.reshape(LEN, HEADS, HEAD_DIM)
        value_seq = value_seq.reshape(LEN, HEADS, HEAD_DIM)
        scores = jnp.einsum('qhd,khd->hqk', query_seq, key_seq, precision=highest_precision) * factor + bias
        scores = lower_precision_backward(scores)
        peak = lax.optimization_barrier(jnp.max(scores, axis=-1, keepdims=True))
        weights = jnp.exp(scores - peak)
        probs = lower_precision(weights / lax.optimization_barrier(jnp.sum(weights, axis=-1, keepdims=True)))
        mixed = jnp.einsum('hqk,khd->qhd', probs, value_seq, precision=highest_precision)
        return mixed.reshape(LEN, D)
    mixed = lax.map(jax.checkpoint(attend), (query_rows, key_rows, value_rows))
    attention_result = lower_precision_backward(lower_precision(mixed))
    second_branch = residual_stream + jnp.einsum('qxm,my->qxy', attention_result, output_projection_weight, precision=highest_precision)
    second_layer_norm = lower_precision(normalize(second_branch, ffn_gain))
    router_logits = jnp.einsum('qxm,my->qxy', second_layer_norm, router, precision=highest_precision)
    probs = jax.nn.softmax(router_logits, axis=-1)
    gate = jnp.take_along_axis(probs, expert_ids[..., None], axis=-1)[..., 0]
    dev_ids = device_rows(expert_ids)
    dev_rows = device_rows(second_layer_norm)
    onehot = (dev_ids[..., None] == jnp.arange(EXPERTS)[None, None, :]).astype(jnp.int32)
    ranks = jnp.cumsum(onehot, axis=1) - 1
    slots = lax.optimization_barrier(jnp.sum(ranks * onehot, axis=-1))
    keep = (slots < CAP).astype(jnp.float32)
    slot_safe = jnp.minimum(slots, CAP - 1)
    device_count = N_DP * N_EXPERT * N_SEQ
    dev_index = jnp.broadcast_to(jnp.arange(device_count)[:, None], dev_ids.shape)
    buffer = jnp.zeros((device_count, EXPERTS, CAP, D), jnp.float32)
    buffer = buffer.at[dev_index, dev_ids, slot_safe].add(dev_rows * keep[..., None])
    buffer = lower_precision_backward(buffer)

    def expert_apply(inputs):
        rows_in, first_weight, second_weight = inputs
        hidden = lower_precision_backward(jnp.einsum('pcd,df->pcf', rows_in, first_weight, precision=highest_precision))
        active = lower_precision(jax.nn.gelu(hidden, approximate=False))
        result = jnp.einsum('pcf,fd->pcd', active, second_weight, precision=highest_precision)
        return lower_precision_backward(lower_precision(result))
    results = lax.map(jax.checkpoint(expert_apply), (jnp.moveaxis(buffer, 1, 0), expert_in, expert_out))
    returned = results[dev_ids, dev_index, slot_safe] * keep[..., None]
    return second_branch + gate[..., None] * from_device_rows(returned)

def reference(tokens, attn_gain, w_query, w_key, w_value, output_projection_weight, bias_table, rel_buckets, ffn_gain, router, expert_in, expert_out, expert_ids, cotangent):

    def closed(residual_stream, gain_one, wq, wk, wv, wo, table, gain_two, route, first, second_branch):
        return forward(residual_stream, gain_one, wq, wk, wv, wo, table, gain_two, route, first, second_branch, rel_buckets, expert_ids)
    params = (tokens.astype(jnp.float32), attn_gain.astype(jnp.float32), w_query.astype(jnp.float32), w_key.astype(jnp.float32), w_value.astype(jnp.float32), output_projection_weight.astype(jnp.float32), bias_table.astype(jnp.float32), ffn_gain.astype(jnp.float32), router.astype(jnp.float32), expert_in.astype(jnp.float32), expert_out.astype(jnp.float32))
    result, pullback = jax.vjp(closed, *params)
    grads = pullback(cotangent.astype(jnp.float32))
    return (result.astype(jnp.bfloat16), grads[0], grads[1], grads[2], grads[3], grads[4], grads[5], grads[6], grads[7], grads[8], grads[9], grads[10])
```

```python
import functools
import math

import jax
import jax.numpy as jnp
from jax import lax
from jax.experimental import pallas as pl
from jax.experimental.pallas import tpu as pltpu
from jax.sharding import PartitionSpec as P

eps = 1e-06
highest_precision = lax.Precision.HIGHEST
lanes = 128
vmem_limit = 56 * 1024 * 1024


def normalize(residual_stream, gain):
    factor = lax.rsqrt(jnp.mean(residual_stream * residual_stream, axis=-1, keepdims=True) + eps)
    return (residual_stream * factor * gain, factor)


def norm_back(grad_norm, residual_stream, factor, gain):
    gain_grad = jnp.sum(grad_norm * residual_stream * factor, axis=0)
    scaled = grad_norm * gain
    inner = jnp.mean(scaled * residual_stream, axis=-1, keepdims=True)
    return (scaled * factor - residual_stream * factor**3 * inner, gain_grad)


def dot_nt(left, right):
    return lax.dot_general(
        left, right, (((1,), (1,)), ((), ())), preferred_element_type=jnp.float32
    )


def dot_tn(left, right):
    return lax.dot_general(
        left, right, (((0,), (0,)), ((), ())), preferred_element_type=jnp.float32
    )


def dot_nn(left, right):
    return jnp.dot(left, right, preferred_element_type=jnp.float32)


def head_part(ref, start, width):
    part = ref[:, 0, :, start : start + width]
    return part.reshape(part.shape[0] * part.shape[1], width)


def attend_kernel(
    heads, head_width, rel_ref, rows_ref, seq_ref, out_ref, probs_ref, skew_ref, keys_ref, values_ref
):
    group = heads * head_width
    block = rows_ref.shape[2]
    length = keys_ref.shape[1]
    step = pl.program_id(1)

    @pl.when((pl.program_id(0) == 0) & (step == 0))
    def build_skew():
        for head in range(heads):
            spread = jnp.broadcast_to(rel_ref[head : head + 1, :], (lanes, 2 * length))
            skew_ref[head] = pltpu.roll(
                spread, 2 * length - (lanes - 1), 1, stride=1, stride_axis=0
            )

    @pl.when(step == 0)
    def split_heads():
        for head in range(heads):
            keys_ref[head] = head_part(seq_ref, group + head * head_width, head_width)
            values_ref[head] = head_part(seq_ref, 2 * group + head * head_width, head_width)

    mixed = []
    for head in range(heads):
        query = rows_ref[0, 0, :, head * head_width : (head + 1) * head_width]
        bias = []
        for sub in range(block // lanes):
            offset = length - lanes - step * block - sub * lanes
            bias.append(skew_ref[head, :, pl.ds(pl.multiple_of(offset, lanes), length)])
        scores = dot_nt(query, keys_ref[head]) * (1.0 / math.sqrt(head_width)) + jnp.concatenate(
            bias, axis=0
        )
        peak = jnp.max(scores, axis=-1, keepdims=True)
        weights = jnp.exp(scores - peak)
        inverse = 1.0 / jnp.sum(weights, axis=-1, keepdims=True)
        rounded = (weights * inverse).astype(jnp.bfloat16)
        probs_ref[0, head] = rounded
        mixed.append(dot_nn(rounded, values_ref[head]))
    out_ref[0, 0] = jnp.concatenate(mixed, axis=-1).astype(jnp.bfloat16)


def attend(rel_pad, qkv, heads, head_width):
    groups, seq_count, piece, triple = qkv.shape
    length = groups * piece
    group = heads * head_width
    pairs = seq_count * heads
    return pl.pallas_call(
        functools.partial(attend_kernel, heads, head_width),
        grid=(seq_count, groups),
        out_shape=(
            jax.ShapeDtypeStruct((groups, seq_count, piece, group), jnp.bfloat16),
            jax.ShapeDtypeStruct((seq_count, heads, length, length), jnp.bfloat16),
        ),
        in_specs=[
            pl.BlockSpec(rel_pad.shape, lambda s, i: (0, 0)),
            pl.BlockSpec((1, 1, piece, triple), lambda s, i: (i, s, 0, 0)),
            pl.BlockSpec((groups, 1, piece, triple), lambda s, i: (0, s, 0, 0)),
        ],
        out_specs=(
            pl.BlockSpec((1, 1, piece, group), lambda s, i: (i, s, 0, 0)),
            pl.BlockSpec((1, heads, piece, length), lambda s, i: (s, 0, i, 0)),
        ),
        scratch_shapes=[
            pltpu.VMEM((heads, lanes, 2 * length), jnp.float32),
            pltpu.VMEM((heads, length, head_width), jnp.bfloat16),
            pltpu.VMEM((heads, length, head_width), jnp.bfloat16),
        ],
        compiler_params=pltpu.CompilerParams(vmem_limit_bytes=vmem_limit),
        cost_estimate=pl.CostEstimate(
            flops=16 * pairs * length * length * head_width,
            bytes_accessed=2 * pairs * length * length,
            transcendentals=pairs * length * length,
        ),
    )(rel_pad, qkv, qkv)


def attend_back_kernel(
    heads,
    head_width,
    rows_ref,
    seq_ref,
    grad_ref,
    probs_ref,
    out_ref,
    rel_ref,
    keys_ref,
    values_ref,
    sums_ref,
    key_grad_ref,
    value_grad_ref,
):
    group = heads * head_width
    groups, _, block, _ = out_ref.shape
    length = keys_ref.shape[1]
    scale = 1.0 / math.sqrt(head_width)
    step = pl.program_id(1)

    @pl.when((pl.program_id(0) == 0) & (step == 0))
    def clear_sums():
        sums_ref[...] = jnp.zeros_like(sums_ref)

    @pl.when(step == 0)
    def split_heads():
        key_grad_ref[...] = jnp.zeros_like(key_grad_ref)
        value_grad_ref[...] = jnp.zeros_like(value_grad_ref)
        for head in range(heads):
            keys_ref[head] = head_part(seq_ref, group + head * head_width, head_width)
            values_ref[head] = head_part(seq_ref, 2 * group + head * head_width, head_width)

    query_turned = rows_ref[0, 0, :, :group].T
    grad_turned = grad_ref[0, 0].T
    query_grads = []
    for head in range(heads):
        span = slice(head * head_width, (head + 1) * head_width)
        grad = grad_ref[0, 0, :, span]
        rounded = probs_ref[0, head]
        weights = rounded.astype(jnp.float32)
        weight_grad = dot_nt(grad, values_ref[head])
        product = weights * weight_grad
        inner = jnp.sum(product, axis=-1, keepdims=True)
        score_grad = product - weights * inner
        score_low = score_grad.astype(jnp.bfloat16)
        for sub in range(block // lanes):
            offset = length - lanes - step * block - sub * lanes
            place = pl.ds(pl.multiple_of(offset, lanes), length)
            sums_ref[head, :, place] += score_grad[sub * lanes : (sub + 1) * lanes]
        query_grads.append(dot_nn(score_low, keys_ref[head]) * scale)
        key_grad_ref[span] += dot_nn(query_turned[span], score_low)
        value_grad_ref[span] += dot_nn(grad_turned[span], rounded)
    out_ref[step, 0, :, :group] = jnp.concatenate(query_grads, axis=-1).astype(jnp.bfloat16)

    @pl.when(step == groups - 1)
    def store_sums():
        key_grad = (key_grad_ref[...] * scale).T.astype(jnp.bfloat16)
        value_grad = value_grad_ref[...].T.astype(jnp.bfloat16)
        out_ref[:, 0, :, group : 2 * group] = key_grad.reshape(groups, block, group)
        out_ref[:, 0, :, 2 * group :] = value_grad.reshape(groups, block, group)

    @pl.when((pl.program_id(0) == pl.num_programs(0) - 1) & (step == groups - 1))
    def fold_sums():
        for head in range(heads):
            folded = sums_ref[head]
            while folded.shape[0] > 1:
                half = folded.shape[0] // 2
                folded = folded[half:] + pltpu.roll(folded[:half], half, 1)
            rel_ref[head : head + 1, :] = folded


def attend_back(qkv, grads, probs, heads, head_width):
    groups, seq_count, piece, triple = qkv.shape
    length = groups * piece
    group = heads * head_width
    pairs = seq_count * heads
    return pl.pallas_call(
        functools.partial(attend_back_kernel, heads, head_width),
        grid=(seq_count, groups),
        out_shape=(
            jax.ShapeDtypeStruct(qkv.shape, jnp.bfloat16),
            jax.ShapeDtypeStruct((heads, 2 * length), jnp.float32),
        ),
        in_specs=[
            pl.BlockSpec((1, 1, piece, triple), lambda s, i: (i, s, 0, 0)),
            pl.BlockSpec((groups, 1, piece, triple), lambda s, i: (0, s, 0, 0)),
            pl.BlockSpec((1, 1, piece, group), lambda s, i: (i, s, 0, 0)),
            pl.BlockSpec((1, heads, piece, length), lambda s, i: (s, 0, i, 0)),
        ],
        out_specs=(
            pl.BlockSpec((groups, 1, piece, triple), lambda s, i: (0, s, 0, 0)),
            pl.BlockSpec((heads, 2 * length), lambda s, i: (0, 0)),
        ),
        scratch_shapes=[
            pltpu.VMEM((heads, length, head_width), jnp.bfloat16),
            pltpu.VMEM((heads, length, head_width), jnp.bfloat16),
            pltpu.VMEM((heads, lanes, 2 * length), jnp.float32),
            pltpu.VMEM((group, length), jnp.float32),
            pltpu.VMEM((group, length), jnp.float32),
        ],
        compiler_params=pltpu.CompilerParams(vmem_limit_bytes=vmem_limit),
        cost_estimate=pl.CostEstimate(
            flops=32 * pairs * length * length * head_width,
            bytes_accessed=2 * pairs * length * length,
            transcendentals=0,
        ),
    )(qkv, qkv, grads, probs)


def expert_kernel(
    width, both_ref, first_ref, second_ref, back_ref, first_grad_ref, second_grad_ref, turned_ref, sum_ref
):
    step = pl.program_id(0)

    @pl.when(step == 0)
    def start_sums():
        sum_ref[...] = jnp.zeros_like(sum_ref)
        turned_ref[...] = both_ref[:, :width].T

    rows = both_ref[:, :width]
    grads = both_ref[:, width:]
    first = first_ref[...]
    second = second_ref[...]
    hidden = dot_nn(rows, first)
    chance = 0.5 + 0.5 * lax.erf(hidden * math.sqrt(0.5))
    active = (hidden * chance).astype(jnp.bfloat16)
    density = jnp.exp(hidden * hidden * -0.5) * (1.0 / math.sqrt(2.0 * math.pi))
    slope = chance + hidden * density
    hidden_grad = (dot_nt(grads, second) * slope).astype(jnp.bfloat16)
    sum_ref[:, :width] += dot_nn(active, second)
    sum_ref[:, width:] += dot_nt(hidden_grad, first)
    second_grad_ref[...] = dot_tn(active, grads).astype(jnp.bfloat16)
    first_grad_ref[...] = dot_nn(turned_ref[...], hidden_grad).astype(jnp.bfloat16)

    @pl.when(step == pl.num_programs(0) - 1)
    def store_sums():
        back_ref[...] = sum_ref[...].astype(jnp.bfloat16)


def expert_layer(both, first, second):
    rows, double = both.shape
    width, hidden_width = first.shape
    block = 512 if hidden_width % 512 == 0 else hidden_width
    return pl.pallas_call(
        functools.partial(expert_kernel, width),
        grid=(hidden_width // block,),
        out_shape=(
            jax.ShapeDtypeStruct(both.shape, jnp.bfloat16),
            jax.ShapeDtypeStruct(first.shape, jnp.bfloat16),
            jax.ShapeDtypeStruct(second.shape, jnp.bfloat16),
        ),
        in_specs=[
            pl.BlockSpec(both.shape, lambda f: (0, 0)),
            pl.BlockSpec((width, block), lambda f: (0, f)),
            pl.BlockSpec((block, width), lambda f: (f, 0)),
        ],
        out_specs=(
            pl.BlockSpec(both.shape, lambda f: (0, 0)),
            pl.BlockSpec((width, block), lambda f: (0, f)),
            pl.BlockSpec((block, width), lambda f: (f, 0)),
        ),
        scratch_shapes=[
            pltpu.VMEM((width, rows), jnp.bfloat16),
            pltpu.VMEM(both.shape, jnp.float32),
        ],
        compiler_params=pltpu.CompilerParams(vmem_limit_bytes=vmem_limit),
        cost_estimate=pl.CostEstimate(
            flops=12 * rows * width * hidden_width,
            bytes_accessed=8 * width * hidden_width,
            transcendentals=2 * rows * hidden_width,
        ),
    )(both, first, second)


def exchange(values, axis):
    return lax.all_to_all(values, axis, split_axis=0, concat_axis=0, tiled=True)


def local(
    tokens,
    attn_gain,
    w_query,
    w_key,
    w_value,
    output_projection_weight,
    bias_table,
    rel_buckets,
    ffn_gain,
    router,
    expert_in,
    expert_out,
    expert_ids,
    cotangent,
):
    seq_count, piece, width = tokens.shape
    groups = lax.axis_size("seq")
    length = piece * groups
    rows = seq_count * piece
    bucket_count, heads_all = bias_table.shape
    local_heads = heads_all // groups
    head_width = width // heads_all
    group_width = local_heads * head_width
    triple = 3 * group_width
    experts = router.shape[1]
    capacity = (5 * rows + 4 * experts - 1) // (4 * experts)
    low = jnp.bfloat16
    high = jnp.float32
    shard_rows = w_query.shape[0]

    def by_group(weight):
        return weight.reshape(shard_rows, groups, group_width).transpose(1, 0, 2)

    projections = jnp.concatenate([by_group(w_query), by_group(w_key), by_group(w_value)], axis=-1)
    full_qkv = lax.all_gather(projections, ("dp", "expert"), axis=1, tiled=True)
    full_output = lax.all_gather(output_projection_weight, ("dp", "expert"), axis=0, tiled=True)
    first_weight = lax.all_gather(expert_in, "dp", axis=1, tiled=True)[0]
    second_weight = lax.all_gather(expert_out, "dp", axis=1, tiled=True)[0]
    output_groups = full_output.reshape(groups, group_width, width)

    residual_stream = tokens.reshape(rows, width).astype(high)
    normed_one, factor_one = normalize(residual_stream, attn_gain)
    first_layer_norm = normed_one.astype(low)
    qkv_rows = jnp.einsum(
        "rm,gmc->grc", first_layer_norm, full_qkv, preferred_element_type=high
    ).astype(low)
    qkv = exchange(qkv_rows.reshape(groups, seq_count, piece, triple), "seq")

    head_start = lax.axis_index("seq") * local_heads
    table_part = lax.dynamic_slice_in_dim(bias_table, head_start, local_heads, 1)
    bucket_onehot = (rel_buckets[:, None] == jnp.arange(bucket_count)[None, :]).astype(high)
    bucket_onehot = jnp.pad(bucket_onehot, ((0, 1), (0, 0)))
    rel_pad = jnp.dot(table_part.T, bucket_onehot.T, precision=highest_precision)
    mixed, probs_kept = attend(rel_pad, qkv, local_heads, head_width)
    attended = exchange(mixed, "seq").reshape(groups, rows, group_width)
    second_branch = residual_stream + jnp.einsum(
        "grc,gcm->rm", attended, output_groups, preferred_element_type=high
    )
    normed_two, factor_two = normalize(second_branch, ffn_gain)
    second_layer_norm = normed_two.astype(low)
    router_logits = jnp.dot(second_layer_norm, router, preferred_element_type=high)
    probs = jax.nn.softmax(router_logits, axis=-1)
    token_ids = expert_ids.reshape(rows)
    onehot = token_ids[:, None] == jnp.arange(experts)[None, :]
    onehot_float = onehot.astype(high)
    gate = jnp.sum(probs * onehot_float, axis=-1)
    earlier = (jnp.arange(rows)[:, None] > jnp.arange(rows)[None, :]).astype(low)
    ranks = jnp.dot(earlier, onehot.astype(low), preferred_element_type=high)
    slots = jnp.sum(ranks * onehot_float, axis=-1).astype(jnp.int32)
    kept = slots < capacity
    keep = kept.astype(high)
    target = jnp.where(kept, token_ids * capacity + slots, -1)
    dispatch = (target[:, None] == jnp.arange(experts * capacity)[None, :]).astype(low)
    out_grad = cotangent.reshape(rows, width).astype(high)
    result_grad = (gate[:, None] * out_grad * keep[:, None]).astype(low)
    outgoing = jnp.concatenate([second_layer_norm, result_grad], axis=-1)
    send = dot_tn(dispatch, outgoing).astype(low)
    received = exchange(send.reshape(experts, capacity, 2 * width), "expert")
    back, first_grad, second_grad = expert_layer(
        received.reshape(experts * capacity, 2 * width), first_weight, second_weight
    )
    returned = exchange(back.reshape(experts, capacity, 2 * width), "expert")
    per_token = dot_nn(dispatch, returned.reshape(experts * capacity, 2 * width))
    token_result = per_token[:, :width]
    layer_out = (second_branch + gate[:, None] * token_result).astype(low)
    gate_grad = jnp.sum(out_grad * token_result, axis=-1)
    logit_grad = probs * (onehot_float * gate_grad[:, None] - (gate * gate_grad)[:, None])
    router_grad = jnp.dot(
        second_layer_norm.astype(high).T, logit_grad, precision=highest_precision
    )
    norm_two_grad = jnp.dot(logit_grad, router.astype(high).T, precision=highest_precision)
    norm_two_grad = norm_two_grad + per_token[:, width:]
    second_back, ffn_gain_grad = norm_back(norm_two_grad, second_branch, factor_two, ffn_gain)
    second_grad_total = out_grad + second_back
    grad_low = second_grad_total.astype(low)
    attended_grad = jnp.einsum(
        "rm,gcm->grc", grad_low, output_groups, preferred_element_type=high
    ).astype(low)
    heads_grad = exchange(attended_grad.reshape(groups, seq_count, piece, group_width), "seq")
    output_weight_grad = jnp.einsum("grc,rm->gcm", attended, grad_low, preferred_element_type=high)
    qkv_back, rel_back = attend_back(qkv, heads_grad, probs_kept, local_heads, head_width)
    table_local = jnp.dot(bucket_onehot.T, rel_back.T, precision=highest_precision)
    table_grad = lax.dynamic_update_slice_in_dim(
        jnp.zeros((bucket_count, heads_all), high), table_local, head_start, 1
    )
    qkv_tok = exchange(qkv_back, "seq").reshape(groups, rows, triple)
    qkv_weight_grad = jnp.einsum(
        "rm,grc->mgc", first_layer_norm, qkv_tok, preferred_element_type=high
    ).astype(low)
    norm_one_grad = jnp.einsum("grc,gmc->rm", qkv_tok, full_qkv, preferred_element_type=high)
    first_back, attn_gain_grad = norm_back(norm_one_grad, residual_stream, factor_one, attn_gain)
    input_grad = second_grad_total + first_back

    first_share = lax.psum(
        lax.psum_scatter(first_grad, "dp", scatter_dimension=0, tiled=True), "seq"
    )
    second_share = lax.psum(
        lax.psum_scatter(second_grad, "dp", scatter_dimension=0, tiled=True), "seq"
    )
    output_share = lax.psum(
        lax.psum_scatter(
            output_weight_grad.reshape(width, width).astype(low),
            ("dp", "expert"),
            scatter_dimension=0,
            tiled=True,
        ),
        "seq",
    )
    qkv_share = lax.psum(
        lax.psum_scatter(
            qkv_weight_grad.reshape(width, groups * triple),
            ("dp", "expert"),
            scatter_dimension=0,
            tiled=True,
        ),
        "seq",
    )
    qkv_share = qkv_share.astype(high).reshape(shard_rows, groups, triple)

    def from_group(part):
        return (
            qkv_share[:, :, part * group_width : (part + 1) * group_width]
            .reshape(shard_rows, width)
        )

    attn_gain_total, ffn_gain_total, router_total, table_total = lax.psum(
        (attn_gain_grad, ffn_gain_grad, router_grad, table_grad), ("dp", "expert", "seq")
    )
    return (
        layer_out.reshape(seq_count, piece, width),
        input_grad.reshape(seq_count, piece, width),
        attn_gain_total,
        from_group(0),
        from_group(1),
        from_group(2),
        output_share.astype(high),
        table_total,
        ffn_gain_total,
        router_total,
        first_share.astype(high)[None],
        second_share.astype(high)[None],
    )


def solution(mesh):
    placed = (
        P(("dp", "expert"), "seq", None),
        P(),
        P(("dp", "expert"), None),
        P(("dp", "expert"), None),
        P(("dp", "expert"), None),
        P(("dp", "expert"), None),
        P(),
        P(),
        P(),
        P(),
        P("expert", "dp", None),
        P("expert", "dp", None),
        P(("dp", "expert"), "seq"),
        P(("dp", "expert"), "seq", None),
    )
    return jax.shard_map(
        local,
        mesh=mesh,
        in_specs=placed,
        out_specs=(
            P(("dp", "expert"), "seq", None),
            P(("dp", "expert"), "seq", None),
            P(),
            P(("dp", "expert"), None),
            P(("dp", "expert"), None),
            P(("dp", "expert"), None),
            P(("dp", "expert"), None),
            P(),
            P(),
            P(),
            P("expert", "dp", None),
            P("expert", "dp", None),
        ),
        check_vma=False,
    )
```

```python
import functools
import math

import jax
import jax.numpy as jnp
from jax import lax
from jax.experimental import pallas as pl
from jax.experimental.pallas import tpu as pltpu
from jax.sharding import PartitionSpec as P

eps = 1e-06
highest_precision = lax.Precision.HIGHEST
lanes = 128
vmem_limit = 56 * 1024 * 1024


def normalize(residual_stream, gain):
    factor = lax.rsqrt(jnp.mean(residual_stream * residual_stream, axis=-1, keepdims=True) + eps)
    return (residual_stream * factor * gain, factor)


def norm_back(grad_norm, residual_stream, factor, gain):
    gain_grad = jnp.sum(grad_norm * residual_stream * factor, axis=0)
    scaled = grad_norm * gain
    inner = jnp.mean(scaled * residual_stream, axis=-1, keepdims=True)
    return (scaled * factor - residual_stream * factor**3 * inner, gain_grad)


def dot_nt(left, right):
    return lax.dot_general(
        left, right, (((1,), (1,)), ((), ())), preferred_element_type=jnp.float32
    )


def dot_tn(left, right):
    return lax.dot_general(
        left, right, (((0,), (0,)), ((), ())), preferred_element_type=jnp.float32
    )


def dot_nn(left, right):
    return jnp.dot(left, right, preferred_element_type=jnp.float32)


def head_part(ref, start, width):
    part = ref[:, 0, :, start : start + width]
    return part.reshape(part.shape[0] * part.shape[1], width)


def attend_kernel(
    heads, head_width, rel_ref, rows_ref, seq_ref, late_ref, out_ref, probs_ref, skew_ref, keys_ref, values_ref
):
    group = heads * head_width
    block = rows_ref.shape[2]
    length = keys_ref.shape[1]
    step = pl.program_id(1)

    @pl.when((pl.program_id(0) == 0) & (step == 0))
    def build_skew():
        for head in range(heads):
            spread = jnp.broadcast_to(rel_ref[head : head + 1, :], (lanes, 2 * length))
            skew_ref[head] = pltpu.roll(
                spread, 2 * length - (lanes - 1), 1, stride=1, stride_axis=0
            )

    @pl.when(step == 0)
    def split_heads():
        for head in range(heads):
            keys_ref[head] = head_part(seq_ref, group + head * head_width, head_width)
            values_ref[head] = head_part(late_ref, head * head_width, head_width)

    mixed = []
    for head in range(heads):
        query = rows_ref[0, 0, :, head * head_width : (head + 1) * head_width]
        bias = []
        for sub in range(block // lanes):
            offset = length - lanes - step * block - sub * lanes
            bias.append(skew_ref[head, :, pl.ds(pl.multiple_of(offset, lanes), length)])
        scores = dot_nt(query, keys_ref[head]) * (1.0 / math.sqrt(head_width)) + jnp.concatenate(
            bias, axis=0
        )
        peak = jnp.max(scores, axis=-1, keepdims=True)
        weights = jnp.exp(scores - peak)
        inverse = 1.0 / jnp.sum(weights, axis=-1, keepdims=True)
        rounded = (weights * inverse).astype(jnp.bfloat16)
        probs_ref[0, head] = rounded
        mixed.append(dot_nn(rounded, values_ref[head]))
    out_ref[0, 0] = jnp.concatenate(mixed, axis=-1).astype(jnp.bfloat16)


def attend(rel_pad, pair, late, heads, head_width):
    groups, seq_count, piece, double = pair.shape
    length = groups * piece
    group = heads * head_width
    pairs = seq_count * heads
    return pl.pallas_call(
        functools.partial(attend_kernel, heads, head_width),
        grid=(seq_count, groups),
        out_shape=(
            jax.ShapeDtypeStruct((groups, seq_count, piece, group), jnp.bfloat16),
            jax.ShapeDtypeStruct((seq_count, heads, length, length), jnp.bfloat16),
        ),
        in_specs=[
            pl.BlockSpec(rel_pad.shape, lambda s, i: (0, 0)),
            pl.BlockSpec((1, 1, piece, double), lambda s, i: (i, s, 0, 0)),
            pl.BlockSpec((groups, 1, piece, double), lambda s, i: (0, s, 0, 0)),
            pl.BlockSpec((groups, 1, piece, group), lambda s, i: (0, s, 0, 0)),
        ],
        out_specs=(
            pl.BlockSpec((1, 1, piece, group), lambda s, i: (i, s, 0, 0)),
            pl.BlockSpec((1, heads, piece, length), lambda s, i: (s, 0, i, 0)),
        ),
        scratch_shapes=[
            pltpu.VMEM((heads, lanes, 2 * length), jnp.float32),
            pltpu.VMEM((heads, length, head_width), jnp.bfloat16),
            pltpu.VMEM((heads, length, head_width), jnp.bfloat16),
        ],
        compiler_params=pltpu.CompilerParams(vmem_limit_bytes=vmem_limit),
        cost_estimate=pl.CostEstimate(
            flops=16 * pairs * length * length * head_width,
            bytes_accessed=2 * pairs * length * length,
            transcendentals=pairs * length * length,
        ),
    )(rel_pad, pair, pair, late)


def attend_back_kernel(
    heads,
    head_width,
    rows_ref,
    seq_ref,
    late_ref,
    grad_ref,
    probs_ref,
    out_ref,
    rel_ref,
    keys_ref,
    values_ref,
    sums_ref,
    key_grad_ref,
    value_grad_ref,
):
    group = heads * head_width
    groups, _, block, _ = out_ref.shape
    length = keys_ref.shape[1]
    scale = 1.0 / math.sqrt(head_width)
    step = pl.program_id(1)

    @pl.when((pl.program_id(0) == 0) & (step == 0))
    def clear_sums():
        sums_ref[...] = jnp.zeros_like(sums_ref)

    @pl.when(step == 0)
    def split_heads():
        key_grad_ref[...] = jnp.zeros_like(key_grad_ref)
        value_grad_ref[...] = jnp.zeros_like(value_grad_ref)
        for head in range(heads):
            keys_ref[head] = head_part(seq_ref, group + head * head_width, head_width)
            values_ref[head] = head_part(late_ref, head * head_width, head_width)

    query_turned = rows_ref[0, 0, :, :group].T
    grad_turned = grad_ref[0, 0].T
    query_grads = []
    for head in range(heads):
        span = slice(head * head_width, (head + 1) * head_width)
        grad = grad_ref[0, 0, :, span]
        rounded = probs_ref[0, head]
        weights = rounded.astype(jnp.float32)
        weight_grad = dot_nt(grad, values_ref[head])
        product = weights * weight_grad
        inner = jnp.sum(product, axis=-1, keepdims=True)
        score_grad = product - weights * inner
        score_low = score_grad.astype(jnp.bfloat16)
        for sub in range(block // lanes):
            offset = length - lanes - step * block - sub * lanes
            place = pl.ds(pl.multiple_of(offset, lanes), length)
            sums_ref[head, :, place] += score_grad[sub * lanes : (sub + 1) * lanes]
        query_grads.append(dot_nn(score_low, keys_ref[head]) * scale)
        key_grad_ref[span] += dot_nn(query_turned[span], score_low)
        value_grad_ref[span] += dot_nn(grad_turned[span], rounded)
    out_ref[step, 0, :, :group] = jnp.concatenate(query_grads, axis=-1).astype(jnp.bfloat16)

    @pl.when(step == groups - 1)
    def store_sums():
        key_grad = (key_grad_ref[...] * scale).T.astype(jnp.bfloat16)
        value_grad = value_grad_ref[...].T.astype(jnp.bfloat16)
        out_ref[:, 0, :, group : 2 * group] = key_grad.reshape(groups, block, group)
        out_ref[:, 0, :, 2 * group :] = value_grad.reshape(groups, block, group)

    @pl.when((pl.program_id(0) == pl.num_programs(0) - 1) & (step == groups - 1))
    def fold_sums():
        for head in range(heads):
            folded = sums_ref[head]
            while folded.shape[0] > 1:
                half = folded.shape[0] // 2
                folded = folded[half:] + pltpu.roll(folded[:half], half, 1)
            rel_ref[head : head + 1, :] = folded


def attend_back(pair, late, grads, probs, heads, head_width):
    groups, seq_count, piece, double = pair.shape
    length = groups * piece
    group = heads * head_width
    pairs = seq_count * heads
    return pl.pallas_call(
        functools.partial(attend_back_kernel, heads, head_width),
        grid=(seq_count, groups),
        out_shape=(
            jax.ShapeDtypeStruct((groups, seq_count, piece, 3 * group), jnp.bfloat16),
            jax.ShapeDtypeStruct((heads, 2 * length), jnp.float32),
        ),
        in_specs=[
            pl.BlockSpec((1, 1, piece, double), lambda s, i: (i, s, 0, 0)),
            pl.BlockSpec((groups, 1, piece, double), lambda s, i: (0, s, 0, 0)),
            pl.BlockSpec((groups, 1, piece, group), lambda s, i: (0, s, 0, 0)),
            pl.BlockSpec((1, 1, piece, group), lambda s, i: (i, s, 0, 0)),
            pl.BlockSpec((1, heads, piece, length), lambda s, i: (s, 0, i, 0)),
        ],
        out_specs=(
            pl.BlockSpec((groups, 1, piece, 3 * group), lambda s, i: (0, s, 0, 0)),
            pl.BlockSpec((heads, 2 * length), lambda s, i: (0, 0)),
        ),
        scratch_shapes=[
            pltpu.VMEM((heads, length, head_width), jnp.bfloat16),
            pltpu.VMEM((heads, length, head_width), jnp.bfloat16),
            pltpu.VMEM((heads, lanes, 2 * length), jnp.float32),
            pltpu.VMEM((group, length), jnp.float32),
            pltpu.VMEM((group, length), jnp.float32),
        ],
        compiler_params=pltpu.CompilerParams(vmem_limit_bytes=vmem_limit),
        cost_estimate=pl.CostEstimate(
            flops=32 * pairs * length * length * head_width,
            bytes_accessed=2 * pairs * length * length,
            transcendentals=0,
        ),
    )(pair, pair, late, grads, probs)


def expert_kernel(
    width, both_ref, first_ref, second_ref, back_ref, first_grad_ref, second_grad_ref, turned_ref, sum_ref
):
    step = pl.program_id(0)

    @pl.when(step == 0)
    def start_sums():
        sum_ref[...] = jnp.zeros_like(sum_ref)
        turned_ref[...] = both_ref[:, :width].T

    rows = both_ref[:, :width]
    grads = both_ref[:, width:]
    first = first_ref[...]
    second = second_ref[...]
    hidden = dot_nn(rows, first)
    chance = 0.5 + 0.5 * lax.erf(hidden * math.sqrt(0.5))
    active = (hidden * chance).astype(jnp.bfloat16)
    density = jnp.exp(hidden * hidden * -0.5) * (1.0 / math.sqrt(2.0 * math.pi))
    slope = chance + hidden * density
    hidden_grad = (dot_nt(grads, second) * slope).astype(jnp.bfloat16)
    sum_ref[:, :width] += dot_nn(active, second)
    sum_ref[:, width:] += dot_nt(hidden_grad, first)
    second_grad_ref[...] = dot_tn(active, grads).astype(jnp.bfloat16)
    first_grad_ref[...] = dot_nn(turned_ref[...], hidden_grad).astype(jnp.bfloat16)

    @pl.when(step == pl.num_programs(0) - 1)
    def store_sums():
        back_ref[...] = sum_ref[...].astype(jnp.bfloat16)


def expert_layer(both, first, second):
    rows, double = both.shape
    width, hidden_width = first.shape
    block = 512 if hidden_width % 512 == 0 else hidden_width
    return pl.pallas_call(
        functools.partial(expert_kernel, width),
        grid=(hidden_width // block,),
        out_shape=(
            jax.ShapeDtypeStruct(both.shape, jnp.bfloat16),
            jax.ShapeDtypeStruct(first.shape, jnp.bfloat16),
            jax.ShapeDtypeStruct(second.shape, jnp.bfloat16),
        ),
        in_specs=[
            pl.BlockSpec(both.shape, lambda f: (0, 0)),
            pl.BlockSpec((width, block), lambda f: (0, f)),
            pl.BlockSpec((block, width), lambda f: (f, 0)),
        ],
        out_specs=(
            pl.BlockSpec(both.shape, lambda f: (0, 0)),
            pl.BlockSpec((width, block), lambda f: (0, f)),
            pl.BlockSpec((block, width), lambda f: (f, 0)),
        ),
        scratch_shapes=[
            pltpu.VMEM((width, rows), jnp.bfloat16),
            pltpu.VMEM(both.shape, jnp.float32),
        ],
        compiler_params=pltpu.CompilerParams(vmem_limit_bytes=vmem_limit),
        cost_estimate=pl.CostEstimate(
            flops=12 * rows * width * hidden_width,
            bytes_accessed=8 * width * hidden_width,
            transcendentals=2 * rows * hidden_width,
        ),
    )(both, first, second)


def exchange(values, axis):
    return lax.all_to_all(values, axis, split_axis=0, concat_axis=0, tiled=True)


def halve_over(values, axis):
    count = lax.axis_size(axis)
    if count & (count - 1):
        return lax.psum_scatter(values, axis, scatter_dimension=0, tiled=True)
    place = lax.axis_index(axis)
    values = values.reshape(count, values.shape[0] // count, values.shape[1])
    bit = 1
    while bit < count:
        own = (place // bit) % 2
        halves = values.reshape(values.shape[0] // 2, 2, *values.shape[1:])
        kept = lax.dynamic_index_in_dim(halves, own, 1, keepdims=False)
        sent = lax.dynamic_index_in_dim(halves, 1 - own, 1, keepdims=False)
        arrived = lax.ppermute(sent, axis, [(i, i ^ bit) for i in range(count)])
        values = (kept.astype(jnp.float32) + arrived.astype(jnp.float32)).astype(jnp.bfloat16)
        bit *= 2
    return values[0]


def local(
    tokens,
    attn_gain,
    w_query,
    w_key,
    w_value,
    output_projection_weight,
    bias_table,
    rel_buckets,
    ffn_gain,
    router,
    expert_in,
    expert_out,
    expert_ids,
    cotangent,
):
    seq_count, piece, width = tokens.shape
    groups = lax.axis_size("seq")
    length = piece * groups
    rows = seq_count * piece
    bucket_count, heads_all = bias_table.shape
    local_heads = heads_all // groups
    head_width = width // heads_all
    group_width = local_heads * head_width
    triple = 3 * group_width
    experts = router.shape[1]
    capacity = (5 * rows + 4 * experts - 1) // (4 * experts)
    low = jnp.bfloat16
    high = jnp.float32
    shard_rows = w_query.shape[0]

    def by_group(weight):
        return weight.reshape(shard_rows, groups, group_width).transpose(1, 0, 2)

    projections = jnp.concatenate([by_group(w_query), by_group(w_key)], axis=-1)
    full_pair = lax.all_gather(projections, ("dp", "expert"), axis=1, tiled=True)
    full_late = lax.all_gather(by_group(w_value), ("dp", "expert"), axis=1, tiled=True)
    full_output = lax.all_gather(output_projection_weight, ("dp", "expert"), axis=0, tiled=True)
    first_weight = lax.all_gather(expert_in, "dp", axis=1, tiled=True)[0]
    second_weight = lax.all_gather(expert_out, "dp", axis=1, tiled=True)[0]
    output_groups = full_output.reshape(groups, group_width, width)

    residual_stream = tokens.reshape(rows, width).astype(high)
    normed_one, factor_one = normalize(residual_stream, attn_gain)
    first_layer_norm = normed_one.astype(low)

    def project(weights):
        projected = jnp.einsum(
            "rm,gmc->grc", first_layer_norm, weights, preferred_element_type=high
        ).astype(low)
        return projected.reshape(groups, seq_count, piece, weights.shape[-1])

    pair = exchange(project(full_pair), "seq")
    late = exchange(project(full_late), "seq")

    head_start = lax.axis_index("seq") * local_heads
    table_part = lax.dynamic_slice_in_dim(bias_table, head_start, local_heads, 1)
    bucket_onehot = (rel_buckets[:, None] == jnp.arange(bucket_count)[None, :]).astype(high)
    bucket_onehot = jnp.pad(bucket_onehot, ((0, 1), (0, 0)))
    rel_pad = jnp.dot(table_part.T, bucket_onehot.T, precision=highest_precision)
    mixed, probs_kept = attend(rel_pad, pair, late, local_heads, head_width)
    attended = exchange(mixed, "seq").reshape(groups, rows, group_width)
    second_branch = residual_stream + jnp.einsum(
        "grc,gcm->rm", attended, output_groups, preferred_element_type=high
    )
    normed_two, factor_two = normalize(second_branch, ffn_gain)
    second_layer_norm = normed_two.astype(low)
    router_logits = jnp.dot(second_layer_norm, router, preferred_element_type=high)
    probs = jax.nn.softmax(router_logits, axis=-1)
    token_ids = expert_ids.reshape(rows)
    onehot = token_ids[:, None] == jnp.arange(experts)[None, :]
    onehot_float = onehot.astype(high)
    gate = jnp.sum(probs * onehot_float, axis=-1)
    earlier = (jnp.arange(rows)[:, None] > jnp.arange(rows)[None, :]).astype(low)
    ranks = jnp.dot(earlier, onehot.astype(low), preferred_element_type=high)
    slots = jnp.sum(ranks * onehot_float, axis=-1).astype(jnp.int32)
    kept = slots < capacity
    keep = kept.astype(high)
    target = jnp.where(kept, token_ids * capacity + slots, -1)
    dispatch = (target[:, None] == jnp.arange(experts * capacity)[None, :]).astype(low)
    out_grad = cotangent.reshape(rows, width).astype(high)
    result_grad = (gate[:, None] * out_grad * keep[:, None]).astype(low)
    outgoing = jnp.concatenate([second_layer_norm, result_grad], axis=-1)
    send = dot_tn(dispatch, outgoing).astype(low)
    received = exchange(send.reshape(experts, capacity, 2 * width), "expert")
    back, first_grad, second_grad = expert_layer(
        received.reshape(experts * capacity, 2 * width), first_weight, second_weight
    )
    returned = exchange(back.reshape(experts, capacity, 2 * width), "expert")
    per_token = dot_nn(dispatch, returned.reshape(experts * capacity, 2 * width))
    token_result = per_token[:, :width]
    layer_out = (second_branch + gate[:, None] * token_result).astype(low)
    gate_grad = jnp.sum(out_grad * token_result, axis=-1)
    logit_grad = probs * (onehot_float * gate_grad[:, None] - (gate * gate_grad)[:, None])
    router_grad = jnp.dot(
        second_layer_norm.astype(high).T, logit_grad, precision=highest_precision
    )
    norm_two_grad = jnp.dot(logit_grad, router.astype(high).T, precision=highest_precision)
    norm_two_grad = norm_two_grad + per_token[:, width:]
    second_back, ffn_gain_grad = norm_back(norm_two_grad, second_branch, factor_two, ffn_gain)
    second_grad_total = out_grad + second_back
    grad_low = second_grad_total.astype(low)
    attended_grad = jnp.einsum(
        "rm,gcm->grc", grad_low, output_groups, preferred_element_type=high
    ).astype(low)
    heads_grad = exchange(attended_grad.reshape(groups, seq_count, piece, group_width), "seq")
    output_weight_grad = jnp.einsum("grc,rm->gcm", attended, grad_low, preferred_element_type=high)
    qkv_back, rel_back = attend_back(pair, late, heads_grad, probs_kept, local_heads, head_width)
    table_local = jnp.dot(bucket_onehot.T, rel_back.T, precision=highest_precision)
    table_grad = lax.dynamic_update_slice_in_dim(
        jnp.zeros((bucket_count, heads_all), high), table_local, head_start, 1
    )
    qkv_tok = exchange(qkv_back, "seq").reshape(groups, rows, triple)
    first_share = halve_over(first_grad, "dp")
    second_share = halve_over(second_grad, "dp")
    output_share = lax.psum_scatter(
        output_weight_grad.reshape(width, width).astype(low),
        ("dp", "expert"),
        scatter_dimension=0,
        tiled=True,
    )
    early_shares = lax.psum((first_share, second_share, output_share), "seq")
    qkv_tok, early_shares = lax.optimization_barrier((qkv_tok, early_shares))
    first_share, second_share, output_share = early_shares
    qkv_weight_grad = jnp.einsum(
        "rm,grc->mgc", first_layer_norm, qkv_tok, preferred_element_type=high
    ).astype(low)
    norm_one_grad = jnp.einsum(
        "grc,gmc->rm", qkv_tok[:, :, : 2 * group_width], full_pair, preferred_element_type=high
    ) + jnp.einsum(
        "grc,gmc->rm", qkv_tok[:, :, 2 * group_width :], full_late, preferred_element_type=high
    )
    first_back, attn_gain_grad = norm_back(norm_one_grad, residual_stream, factor_one, attn_gain)
    input_grad = second_grad_total + first_back

    qkv_share = lax.psum_scatter(
        qkv_weight_grad, ("dp", "expert"), scatter_dimension=0, tiled=True
    )
    small_totals = lax.psum(
        (attn_gain_grad, ffn_gain_grad, router_grad, table_grad), ("dp", "expert", "seq")
    )
    qkv_share, small_totals = lax.optimization_barrier((qkv_share, small_totals))
    attn_gain_total, ffn_gain_total, router_total, table_total = small_totals
    qkv_share = lax.psum(qkv_share, "seq").astype(high)

    def from_group(part):
        return (
            qkv_share[:, :, part * group_width : (part + 1) * group_width]
            .reshape(shard_rows, width)
        )

    return (
        layer_out.reshape(seq_count, piece, width),
        input_grad.reshape(seq_count, piece, width),
        attn_gain_total,
        from_group(0),
        from_group(1),
        from_group(2),
        output_share.astype(high),
        table_total,
        ffn_gain_total,
        router_total,
        first_share.astype(high)[None],
        second_share.astype(high)[None],
    )


def solution(mesh):
    placed = (
        P(("dp", "expert"), "seq", None),
        P(),
        P(("dp", "expert"), None),
        P(("dp", "expert"), None),
        P(("dp", "expert"), None),
        P(("dp", "expert"), None),
        P(),
        P(),
        P(),
        P(),
        P("expert", "dp", None),
        P("expert", "dp", None),
        P(("dp", "expert"), "seq"),
        P(("dp", "expert"), "seq", None),
    )
    return jax.shard_map(
        local,
        mesh=mesh,
        in_specs=placed,
        out_specs=(
            P(("dp", "expert"), "seq", None),
            P(("dp", "expert"), "seq", None),
            P(),
            P(("dp", "expert"), None),
            P(("dp", "expert"), None),
            P(("dp", "expert"), None),
            P(("dp", "expert"), None),
            P(),
            P(),
            P(),
            P("expert", "dp", None),
            P("expert", "dp", None),
        ),
        check_vma=False,
    )
```

```python
import functools
import math

import jax
import jax.numpy as jnp
from jax import lax
from jax.experimental import pallas as pl
from jax.experimental.pallas import tpu as pltpu
from jax.sharding import PartitionSpec as P

eps = 1e-06
highest_precision = lax.Precision.HIGHEST
lanes = 128
vmem_limit = 56 * 1024 * 1024


def normalize(residual_stream, gain):
    factor = lax.rsqrt(jnp.mean(residual_stream * residual_stream, axis=-1, keepdims=True) + eps)
    return (residual_stream * factor * gain, factor)


def norm_back(grad_norm, residual_stream, factor, gain):
    gain_grad = jnp.sum(grad_norm * residual_stream * factor, axis=0)
    scaled = grad_norm * gain
    inner = jnp.mean(scaled * residual_stream, axis=-1, keepdims=True)
    return (scaled * factor - residual_stream * factor**3 * inner, gain_grad)


def dot_nt(left, right):
    return lax.dot_general(
        left, right, (((1,), (1,)), ((), ())), preferred_element_type=jnp.float32
    )


def dot_tn(left, right):
    return lax.dot_general(
        left, right, (((0,), (0,)), ((), ())), preferred_element_type=jnp.float32
    )


def dot_nn(left, right):
    return jnp.dot(left, right, preferred_element_type=jnp.float32)


def head_part(ref, start, width):
    part = ref[:, 0, :, start : start + width]
    return part.reshape(part.shape[0] * part.shape[1], width)


def attend_kernel(
    heads, head_width, rel_ref, rows_ref, seq_ref, out_ref, probs_ref, skew_ref, keys_ref, values_ref
):
    group = heads * head_width
    block = rows_ref.shape[2]
    length = keys_ref.shape[1]
    step = pl.program_id(1)

    @pl.when((pl.program_id(0) == 0) & (step == 0))
    def build_skew():
        for head in range(heads):
            spread = jnp.broadcast_to(rel_ref[head : head + 1, :], (lanes, 2 * length))
            skew_ref[head] = pltpu.roll(
                spread, 2 * length - (lanes - 1), 1, stride=1, stride_axis=0
            )

    @pl.when(step == 0)
    def split_heads():
        for head in range(heads):
            keys_ref[head] = head_part(seq_ref, group + head * head_width, head_width)
            values_ref[head] = head_part(seq_ref, 2 * group + head * head_width, head_width)

    mixed = []
    for head in range(heads):
        query = rows_ref[0, 0, :, head * head_width : (head + 1) * head_width]
        bias = []
        for sub in range(block // lanes):
            offset = length - lanes - step * block - sub * lanes
            bias.append(skew_ref[head, :, pl.ds(pl.multiple_of(offset, lanes), length)])
        scores = dot_nt(query, keys_ref[head]) * (1.0 / math.sqrt(head_width)) + jnp.concatenate(
            bias, axis=0
        )
        peak = jnp.max(scores, axis=-1, keepdims=True)
        weights = jnp.exp(scores - peak)
        inverse = 1.0 / jnp.sum(weights, axis=-1, keepdims=True)
        rounded = (weights * inverse).astype(jnp.bfloat16)
        probs_ref[0, head] = rounded
        mixed.append(dot_nn(rounded, values_ref[head]))
    out_ref[0, 0] = jnp.concatenate(mixed, axis=-1).astype(jnp.bfloat16)


def attend(rel_pad, qkv, heads, head_width):
    groups, seq_count, piece, triple = qkv.shape
    length = groups * piece
    group = heads * head_width
    pairs = seq_count * heads
    return pl.pallas_call(
        functools.partial(attend_kernel, heads, head_width),
        grid=(seq_count, groups),
        out_shape=(
            jax.ShapeDtypeStruct((groups, seq_count, piece, group), jnp.bfloat16),
            jax.ShapeDtypeStruct((seq_count, heads, length, length), jnp.bfloat16),
        ),
        in_specs=[
            pl.BlockSpec(rel_pad.shape, lambda s, i: (0, 0)),
            pl.BlockSpec((1, 1, piece, triple), lambda s, i: (i, s, 0, 0)),
            pl.BlockSpec((groups, 1, piece, triple), lambda s, i: (0, s, 0, 0)),
        ],
        out_specs=(
            pl.BlockSpec((1, 1, piece, group), lambda s, i: (i, s, 0, 0)),
            pl.BlockSpec((1, heads, piece, length), lambda s, i: (s, 0, i, 0)),
        ),
        scratch_shapes=[
            pltpu.VMEM((heads, lanes, 2 * length), jnp.float32),
            pltpu.VMEM((heads, length, head_width), jnp.bfloat16),
            pltpu.VMEM((heads, length, head_width), jnp.bfloat16),
        ],
        compiler_params=pltpu.CompilerParams(vmem_limit_bytes=vmem_limit),
        cost_estimate=pl.CostEstimate(
            flops=16 * pairs * length * length * head_width,
            bytes_accessed=2 * pairs * length * length,
            transcendentals=pairs * length * length,
        ),
    )(rel_pad, qkv, qkv)


def attend_back_kernel(
    heads,
    head_width,
    rows_ref,
    seq_ref,
    grad_ref,
    probs_ref,
    out_ref,
    rel_ref,
    keys_ref,
    values_ref,
    sums_ref,
    key_grad_ref,
    value_grad_ref,
):
    group = heads * head_width
    groups, _, block, _ = out_ref.shape
    length = keys_ref.shape[1]
    scale = 1.0 / math.sqrt(head_width)
    step = pl.program_id(1)

    @pl.when((pl.program_id(0) == 0) & (step == 0))
    def clear_sums():
        sums_ref[...] = jnp.zeros_like(sums_ref)

    @pl.when(step == 0)
    def split_heads():
        key_grad_ref[...] = jnp.zeros_like(key_grad_ref)
        value_grad_ref[...] = jnp.zeros_like(value_grad_ref)
        for head in range(heads):
            keys_ref[head] = head_part(seq_ref, group + head * head_width, head_width)
            values_ref[head] = head_part(seq_ref, 2 * group + head * head_width, head_width)

    query_turned = rows_ref[0, 0, :, :group].T
    grad_turned = grad_ref[0, 0].T
    query_grads = []
    for head in range(heads):
        span = slice(head * head_width, (head + 1) * head_width)
        grad = grad_ref[0, 0, :, span]
        rounded = probs_ref[0, head]
        weights = rounded.astype(jnp.float32)
        weight_grad = dot_nt(grad, values_ref[head])
        product = weights * weight_grad
        inner = jnp.sum(product, axis=-1, keepdims=True)
        score_grad = product - weights * inner
        score_low = score_grad.astype(jnp.bfloat16)
        for sub in range(block // lanes):
            offset = length - lanes - step * block - sub * lanes
            place = pl.ds(pl.multiple_of(offset, lanes), length)
            sums_ref[head, :, place] += score_grad[sub * lanes : (sub + 1) * lanes]
        query_grads.append(dot_nn(score_low, keys_ref[head]) * scale)
        key_grad_ref[span] += dot_nn(query_turned[span], score_low)
        value_grad_ref[span] += dot_nn(grad_turned[span], rounded)
    out_ref[step, 0, :, :group] = jnp.concatenate(query_grads, axis=-1).astype(jnp.bfloat16)

    @pl.when(step == groups - 1)
    def store_sums():
        key_grad = (key_grad_ref[...] * scale).T.astype(jnp.bfloat16)
        value_grad = value_grad_ref[...].T.astype(jnp.bfloat16)
        out_ref[:, 0, :, group : 2 * group] = key_grad.reshape(groups, block, group)
        out_ref[:, 0, :, 2 * group :] = value_grad.reshape(groups, block, group)

    @pl.when((pl.program_id(0) == pl.num_programs(0) - 1) & (step == groups - 1))
    def fold_sums():
        for head in range(heads):
            folded = sums_ref[head]
            while folded.shape[0] > 1:
                half = folded.shape[0] // 2
                folded = folded[half:] + pltpu.roll(folded[:half], half, 1)
            rel_ref[head : head + 1, :] = folded


def attend_back(qkv, grads, probs, heads, head_width):
    groups, seq_count, piece, triple = qkv.shape
    length = groups * piece
    group = heads * head_width
    pairs = seq_count * heads
    return pl.pallas_call(
        functools.partial(attend_back_kernel, heads, head_width),
        grid=(seq_count, groups),
        out_shape=(
            jax.ShapeDtypeStruct((groups, seq_count, piece, 3 * group), jnp.bfloat16),
            jax.ShapeDtypeStruct((heads, 2 * length), jnp.float32),
        ),
        in_specs=[
            pl.BlockSpec((1, 1, piece, triple), lambda s, i: (i, s, 0, 0)),
            pl.BlockSpec((groups, 1, piece, triple), lambda s, i: (0, s, 0, 0)),
            pl.BlockSpec((1, 1, piece, group), lambda s, i: (i, s, 0, 0)),
            pl.BlockSpec((1, heads, piece, length), lambda s, i: (s, 0, i, 0)),
        ],
        out_specs=(
            pl.BlockSpec((groups, 1, piece, 3 * group), lambda s, i: (0, s, 0, 0)),
            pl.BlockSpec((heads, 2 * length), lambda s, i: (0, 0)),
        ),
        scratch_shapes=[
            pltpu.VMEM((heads, length, head_width), jnp.bfloat16),
            pltpu.VMEM((heads, length, head_width), jnp.bfloat16),
            pltpu.VMEM((heads, lanes, 2 * length), jnp.float32),
            pltpu.VMEM((group, length), jnp.float32),
            pltpu.VMEM((group, length), jnp.float32),
        ],
        compiler_params=pltpu.CompilerParams(vmem_limit_bytes=vmem_limit),
        cost_estimate=pl.CostEstimate(
            flops=32 * pairs * length * length * head_width,
            bytes_accessed=2 * pairs * length * length,
            transcendentals=0,
        ),
    )(qkv, qkv, grads, probs)


def expert_kernel(
    width, both_ref, first_ref, second_ref, back_ref, first_grad_ref, second_grad_ref, turned_ref, sum_ref
):
    step = pl.program_id(0)

    @pl.when(step == 0)
    def start_sums():
        sum_ref[...] = jnp.zeros_like(sum_ref)
        turned_ref[...] = both_ref[:, :width].T

    rows = both_ref[:, :width]
    grads = both_ref[:, width:]
    first = first_ref[...]
    second = second_ref[...]
    hidden = dot_nn(rows, first)
    chance = 0.5 + 0.5 * lax.erf(hidden * math.sqrt(0.5))
    active = (hidden * chance).astype(jnp.bfloat16)
    density = jnp.exp(hidden * hidden * -0.5) * (1.0 / math.sqrt(2.0 * math.pi))
    slope = chance + hidden * density
    hidden_grad = (dot_nt(grads, second) * slope).astype(jnp.bfloat16)
    sum_ref[:, :width] += dot_nn(active, second)
    sum_ref[:, width:] += dot_nt(hidden_grad, first)
    second_grad_ref[...] = dot_tn(active, grads).astype(jnp.bfloat16)
    first_grad_ref[...] = dot_nn(turned_ref[...], hidden_grad).astype(jnp.bfloat16)

    @pl.when(step == pl.num_programs(0) - 1)
    def store_sums():
        back_ref[...] = sum_ref[...].astype(jnp.bfloat16)


def expert_layer(both, first, second):
    rows, double = both.shape
    width, hidden_width = first.shape
    block = 512 if hidden_width % 512 == 0 else hidden_width
    return pl.pallas_call(
        functools.partial(expert_kernel, width),
        grid=(hidden_width // block,),
        out_shape=(
            jax.ShapeDtypeStruct(both.shape, jnp.bfloat16),
            jax.ShapeDtypeStruct(first.shape, jnp.bfloat16),
            jax.ShapeDtypeStruct(second.shape, jnp.bfloat16),
        ),
        in_specs=[
            pl.BlockSpec(both.shape, lambda f: (0, 0)),
            pl.BlockSpec((width, block), lambda f: (0, f)),
            pl.BlockSpec((block, width), lambda f: (f, 0)),
        ],
        out_specs=(
            pl.BlockSpec(both.shape, lambda f: (0, 0)),
            pl.BlockSpec((width, block), lambda f: (0, f)),
            pl.BlockSpec((block, width), lambda f: (f, 0)),
        ),
        scratch_shapes=[
            pltpu.VMEM((width, rows), jnp.bfloat16),
            pltpu.VMEM(both.shape, jnp.float32),
        ],
        compiler_params=pltpu.CompilerParams(vmem_limit_bytes=vmem_limit),
        cost_estimate=pl.CostEstimate(
            flops=12 * rows * width * hidden_width,
            bytes_accessed=8 * width * hidden_width,
            transcendentals=2 * rows * hidden_width,
        ),
    )(both, first, second)


def exchange(values, axis):
    return lax.all_to_all(values, axis, split_axis=0, concat_axis=0, tiled=True)


def halve_over(values, axis):
    count = lax.axis_size(axis)
    if count & (count - 1):
        return lax.psum_scatter(values, axis, scatter_dimension=0, tiled=True)
    place = lax.axis_index(axis)
    values = values.reshape(count, values.shape[0] // count, *values.shape[1:])
    bit = 1
    while bit < count:
        own = (place // bit) % 2
        halves = values.reshape(values.shape[0] // 2, 2, *values.shape[1:])
        kept = lax.dynamic_index_in_dim(halves, own, 1, keepdims=False)
        sent = lax.dynamic_index_in_dim(halves, 1 - own, 1, keepdims=False)
        arrived = lax.ppermute(sent, axis, [(i, i ^ bit) for i in range(count)])
        values = (kept.astype(jnp.float32) + arrived.astype(jnp.float32)).astype(jnp.bfloat16)
        bit *= 2
    return values[0]


def local(
    tokens,
    attn_gain,
    w_query,
    w_key,
    w_value,
    output_projection_weight,
    bias_table,
    rel_buckets,
    ffn_gain,
    router,
    expert_in,
    expert_out,
    expert_ids,
    cotangent,
):
    seq_count, piece, width = tokens.shape
    groups = lax.axis_size("seq")
    length = piece * groups
    rows = seq_count * piece
    bucket_count, heads_all = bias_table.shape
    local_heads = heads_all // groups
    head_width = width // heads_all
    group_width = local_heads * head_width
    triple = 3 * group_width
    experts = router.shape[1]
    capacity = (5 * rows + 4 * experts - 1) // (4 * experts)
    low = jnp.bfloat16
    high = jnp.float32
    shard_rows = w_query.shape[0]

    def by_group(weight):
        return weight.reshape(shard_rows, groups, group_width).transpose(1, 0, 2)

    projections = jnp.concatenate([by_group(w_query), by_group(w_key), by_group(w_value)], axis=-1)
    full_qkv = lax.all_gather(projections, ("dp", "expert"), axis=1, tiled=True)
    full_output = lax.all_gather(output_projection_weight, ("dp", "expert"), axis=0, tiled=True)
    first_weight = lax.all_gather(expert_in, "dp", axis=1, tiled=True)[0]
    second_weight = lax.all_gather(expert_out, "dp", axis=1, tiled=True)[0]
    output_groups = full_output.reshape(groups, group_width, width)

    residual_stream = tokens.reshape(rows, width).astype(high)
    normed_one, factor_one = normalize(residual_stream, attn_gain)
    first_layer_norm = normed_one.astype(low)
    qkv_rows = jnp.einsum(
        "rm,gmc->grc", first_layer_norm, full_qkv, preferred_element_type=high
    ).astype(low)
    qkv = exchange(qkv_rows.reshape(groups, seq_count, piece, triple), "seq")

    head_start = lax.axis_index("seq") * local_heads
    table_part = lax.dynamic_slice_in_dim(bias_table, head_start, local_heads, 1)
    bucket_onehot = (rel_buckets[:, None] == jnp.arange(bucket_count)[None, :]).astype(high)
    bucket_onehot = jnp.pad(bucket_onehot, ((0, 1), (0, 0)))
    rel_pad = jnp.dot(table_part.T, bucket_onehot.T, precision=highest_precision)
    mixed, probs_kept = attend(rel_pad, qkv, local_heads, head_width)
    attended = exchange(mixed, "seq").reshape(groups, rows, group_width)
    second_branch = residual_stream + jnp.einsum(
        "grc,gcm->rm", attended, output_groups, preferred_element_type=high
    )
    normed_two, factor_two = normalize(second_branch, ffn_gain)
    second_layer_norm = normed_two.astype(low)
    router_logits = jnp.dot(second_layer_norm, router, preferred_element_type=high)
    probs = jax.nn.softmax(router_logits, axis=-1)
    token_ids = expert_ids.reshape(rows)
    onehot = token_ids[:, None] == jnp.arange(experts)[None, :]
    onehot_float = onehot.astype(high)
    gate = jnp.sum(probs * onehot_float, axis=-1)
    earlier = (jnp.arange(rows)[:, None] > jnp.arange(rows)[None, :]).astype(low)
    ranks = jnp.dot(earlier, onehot.astype(low), preferred_element_type=high)
    slots = jnp.sum(ranks * onehot_float, axis=-1).astype(jnp.int32)
    kept = slots < capacity
    keep = kept.astype(high)
    target = jnp.where(kept, token_ids * capacity + slots, -1)
    dispatch = (target[:, None] == jnp.arange(experts * capacity)[None, :]).astype(low)
    out_grad = cotangent.reshape(rows, width).astype(high)
    result_grad = (gate[:, None] * out_grad * keep[:, None]).astype(low)
    outgoing = jnp.concatenate([second_layer_norm, result_grad], axis=-1)
    send = dot_tn(dispatch, outgoing).astype(low)
    received = exchange(send.reshape(experts, capacity, 2 * width), "expert")
    back, first_grad, second_grad = expert_layer(
        received.reshape(experts * capacity, 2 * width), first_weight, second_weight
    )
    returned = exchange(back.reshape(experts, capacity, 2 * width), "expert")
    per_token = dot_nn(dispatch, returned.reshape(experts * capacity, 2 * width))
    token_result = per_token[:, :width]
    layer_out = (second_branch + gate[:, None] * token_result).astype(low)
    gate_grad = jnp.sum(out_grad * token_result, axis=-1)
    logit_grad = probs * (onehot_float * gate_grad[:, None] - (gate * gate_grad)[:, None])
    router_grad = jnp.dot(
        second_layer_norm.astype(high).T, logit_grad, precision=highest_precision
    )
    norm_two_grad = jnp.dot(logit_grad, router.astype(high).T, precision=highest_precision)
    norm_two_grad = norm_two_grad + per_token[:, width:]
    second_back, ffn_gain_grad = norm_back(norm_two_grad, second_branch, factor_two, ffn_gain)
    second_grad_total = out_grad + second_back
    grad_low = second_grad_total.astype(low)
    attended_grad = jnp.einsum(
        "rm,gcm->grc", grad_low, output_groups, preferred_element_type=high
    ).astype(low)
    heads_grad = exchange(attended_grad.reshape(groups, seq_count, piece, group_width), "seq")
    output_weight_grad = jnp.einsum("grc,rm->gcm", attended, grad_low, preferred_element_type=high)
    qkv_back, rel_back = attend_back(qkv, heads_grad, probs_kept, local_heads, head_width)
    table_local = jnp.dot(bucket_onehot.T, rel_back.T, precision=highest_precision)
    table_grad = lax.dynamic_update_slice_in_dim(
        jnp.zeros((bucket_count, heads_all), high), table_local, head_start, 1
    )
    qkv_tok = exchange(qkv_back, "seq").reshape(groups, rows, triple)
    first_share = halve_over(first_grad, "dp")
    second_share = halve_over(second_grad, "dp")
    output_share = lax.psum_scatter(
        output_weight_grad.reshape(width, width).astype(low),
        ("dp", "expert"),
        scatter_dimension=0,
        tiled=True,
    )
    qkv_tok, shares = lax.optimization_barrier(
        (qkv_tok, (first_share, second_share, output_share))
    )
    early_shares = lax.psum(shares, "seq")
    qkv_weight_grad = jnp.einsum(
        "rm,grc->mgc", first_layer_norm, qkv_tok, preferred_element_type=high
    ).astype(low)
    norm_one_grad = jnp.einsum("grc,gmc->rm", qkv_tok, full_qkv, preferred_element_type=high)
    first_back, attn_gain_grad = norm_back(norm_one_grad, residual_stream, factor_one, attn_gain)
    input_grad = second_grad_total + first_back

    qkv_share = halve_over(halve_over(qkv_weight_grad, "dp"), "expert")
    qkv_share, small_sums = lax.optimization_barrier(
        (qkv_share, (attn_gain_grad, ffn_gain_grad, router_grad, table_grad))
    )
    attn_gain_total, ffn_gain_total, router_total, table_total = lax.psum(
        small_sums, ("dp", "expert", "seq")
    )
    qkv_share, early_shares = lax.optimization_barrier((qkv_share, early_shares))
    first_share, second_share, output_share = early_shares
    qkv_share = lax.psum(qkv_share, "seq").astype(high)

    def from_group(part):
        return (
            qkv_share[:, :, part * group_width : (part + 1) * group_width]
            .reshape(shard_rows, width)
        )

    return (
        layer_out.reshape(seq_count, piece, width),
        input_grad.reshape(seq_count, piece, width),
        attn_gain_total,
        from_group(0),
        from_group(1),
        from_group(2),
        output_share.astype(high),
        table_total,
        ffn_gain_total,
        router_total,
        first_share.astype(high)[None],
        second_share.astype(high)[None],
    )


def solution(mesh):
    placed = (
        P(("dp", "expert"), "seq", None),
        P(),
        P(("dp", "expert"), None),
        P(("dp", "expert"), None),
        P(("dp", "expert"), None),
        P(("dp", "expert"), None),
        P(),
        P(),
        P(),
        P(),
        P("expert", "dp", None),
        P("expert", "dp", None),
        P(("dp", "expert"), "seq"),
        P(("dp", "expert"), "seq", None),
    )
    return jax.shard_map(
        local,
        mesh=mesh,
        in_specs=placed,
        out_specs=(
            P(("dp", "expert"), "seq", None),
            P(("dp", "expert"), "seq", None),
            P(),
            P(("dp", "expert"), None),
            P(("dp", "expert"), None),
            P(("dp", "expert"), None),
            P(("dp", "expert"), None),
            P(),
            P(),
            P(),
            P("expert", "dp", None),
            P("expert", "dp", None),
        ),
        check_vma=False,
    )
```
